32 devices in a mesh: pipe: 4 (over z), blk: 2 (over x), uly: 4 (over y, core).
Axes of the slice: x: 2, y: 2, z: 4, core: 2. Of those that a mesh axis runs over, the one named last changes fastest.
Arguments:
- hidden_in: bfloat16 [4, 64, 3072], P('pipe', ('blk', 'uly')), may hold values from -6 to 6
- text_len: int32 [1], replicated, may hold values from 16 to 64
- qkv_video: bfloat16 [4, 3072, 3, 1536], P('pipe', 'blk', None, 'uly'), may hold values from -0.109375 to 0.109375
- qkv_text: bfloat16 [2, 3072, 3, 1536], P(None, 'blk', None, 'uly'), may hold values from -0.109375 to 0.109375
- out_video: bfloat16 [4, 1536, 3072], P('pipe', 'uly', 'blk'), may hold values from -0.15625 to 0.15625
- out_text: bfloat16 [2, 1536, 3072], P(None, 'uly', 'blk'), may hold values from -0.15625 to 0.15625
- modulation: float32 [4, 2, 3, 3072], P('pipe'), may hold values from -3 to 3
- qk_gain: float32 [4, 2, 2, 128], P('pipe'), may hold values from 1 to 3
- stale_kv: bfloat16 [4, 2, 256, 1536], P('pipe', None, None, 'uly'), may hold values from -24 to 24, as said below
Outputs:
- hidden_out: bfloat16 [4, 64, 3072], P('pipe', ('blk', 'uly'))
The draws below stay inside these ranges and needn't reach their ends.
Inputs may be any that keep to these rules, and one draw needn't show every extreme that they name: `stale_kv`: stale keys and values of order one, some keys larger.
All inputs are finite; a program needn't handle non-finite values.
Results may differ from the reference program's by a relative error of at most 0.04.
Values may be sent and summed in bfloat16 or wider, within the bound.
A program may use at most 128 MiB of HBM per device.

```python
import math
import jax
import jax.numpy as jnp
from jax import lax

D = 3072
HEADS = 12
HD = 128
HW = 1536
NDUAL = 2
ST = 64
P_SIZE = 64
L = 256
N_PIPE = 4


def draw_stale_kv(key, part):
    shape = (N_PIPE, 2, L, HW)
    base = 1.5 * jax.random.normal(key, shape, jnp.float32)
    return jnp.clip(base, -9.0, 9.0).astype(jnp.bfloat16)


def block_levels(key, shape, cuts, least, largest):
    factor_of = 1.0
    for dim, shards_of in cuts:
        steps = jax.random.uniform(jax.random.fold_in(jax.random.fold_in(key, 6), dim), (shards_of,), jnp.float32, least / len(cuts), largest / len(cuts))
        factor_of = factor_of * jnp.repeat(jnp.exp(steps), shape[dim] // shards_of).reshape((-1,) + (1,) * (len(shape) - 1 - dim))
    return factor_of


def scatter_about(rng, shape, deviation, reach, split=(), kind=jnp.bfloat16):
    drawn = jax.random.normal(rng, shape, jnp.float32) * deviation
    if len(split) > 0:
        drawn = block_levels(rng, shape, split, -0.22, 0.18) * drawn
    return jnp.clip(drawn, min=-reach, max=reach).astype(kind)


def setup_inputs(seed: int = 0) -> dict:
    key_list = jax.random.split(jax.random.key(seed), 10)
    return {
        "hidden_in": scatter_about(key_list[0], (N_PIPE, P_SIZE, D), 1.0, 6.0, ((0, 4), (1, 8))),
        "text_len": jax.random.randint(key_list[1], (1,), ST // 4, ST + 1).astype(jnp.int32),
        "qkv_video": scatter_about(key_list[2], (N_PIPE, D, 3, HW), D ** -0.5, 0.109375, ((0, 4), (1, 2), (3, 4))),
        "qkv_text": scatter_about(key_list[3], (NDUAL, D, 3, HW), D ** -0.5, 0.109375, ((1, 2), (3, 4))),
        "out_video": scatter_about(key_list[4], (N_PIPE, HW, D), HW ** -0.5, 0.15625, ((0, 4), (1, 4), (2, 2))),
        "out_text": scatter_about(key_list[5], (NDUAL, HW, D), HW ** -0.5, 0.15625, ((1, 4), (2, 2))),
        "modulation": scatter_about(key_list[6], (N_PIPE, 2, 3, D), 0.5, 3.0, ((0, 4),), jnp.float32),
        "qk_gain": jnp.clip(jnp.exp(math.log(3.0) - 1.0986123 * jax.random.uniform(key_list[7], (N_PIPE, 2, 2, HD), jnp.float32) ** block_levels(key_list[7], (N_PIPE, 2, 2, HD), ((0, 4),), -0.2, 0.2)), 1.0, 3.0),
        "stale_kv": draw_stale_kv(jax.random.fold_in(key_list[9], 71), 0),
    }


def rms_scale(values, gain):
    squares = lax.optimization_barrier(jnp.mean(values * values, axis=-1, keepdims=True))
    return values * lax.rsqrt(squares + 1e-06) * gain

def reference(hidden_in, text_len, qkv_video, qkv_text, out_video, out_text, modulation, qk_gain, stale_kv):
    hidden = hidden_in.reshape(N_PIPE * P_SIZE, D)
    places = jnp.arange(L, dtype=jnp.int32)
    key_ok = (places >= ST) | (places < text_len[0])
    inv_scale = 1.0 / math.sqrt(HD)
    for block in range(N_PIPE):
        dual = block < NDUAL
        cache_keys = stale_kv[block, 0]
        cache_values = stale_kv[block, 1]
        pieces = []
        mods = modulation[block]
        gains = qk_gain[block]
        for micro in range(N_PIPE):
            rows = hidden[micro * P_SIZE:(micro + 1) * P_SIZE]
            tokens = micro * P_SIZE + jnp.arange(P_SIZE, dtype=jnp.int32)
            if dual:
                is_text = (tokens < ST)[:, None]
            else:
                is_text = jnp.zeros((P_SIZE, 1), dtype=bool)
            shift_rows = jnp.where(is_text, mods[1, 0], mods[0, 0])
            scale_rows = jnp.where(is_text, mods[1, 1], mods[0, 1])
            gate_rows = jnp.where(is_text, mods[1, 2], mods[0, 2])
            floats = rows.astype(jnp.float32)
            centred = floats - lax.optimization_barrier(jnp.mean(floats, axis=-1, keepdims=True))
            normed = centred * lax.rsqrt(lax.optimization_barrier(jnp.mean(centred * centred, axis=-1, keepdims=True)) + 1e-06)
            modded = (normed * (1.0 + scale_rows) + shift_rows).astype(jnp.bfloat16)
            projected = jnp.dot(modded, qkv_video[block].reshape(D, 3 * HW), preferred_element_type=jnp.float32)
            if dual:
                text_part = jnp.dot(modded, qkv_text[block].reshape(D, 3 * HW), preferred_element_type=jnp.float32)
                projected = jnp.where(is_text, text_part, projected)
            projected = projected.reshape(P_SIZE, 3, HEADS, HD)
            text_heads = is_text[:, :, None]
            query_gain = jnp.where(text_heads, gains[1, 0], gains[0, 0])
            key_gain = jnp.where(text_heads, gains[1, 1], gains[0, 1])
            queries = rms_scale(projected[:, 0], query_gain).astype(jnp.bfloat16)
            fresh_keys = rms_scale(projected[:, 1], key_gain).astype(jnp.bfloat16)
            fresh_values = projected[:, 2].astype(jnp.bfloat16)
            cache_keys = cache_keys.at[micro * P_SIZE:(micro + 1) * P_SIZE].set(fresh_keys.reshape(P_SIZE, HW))
            cache_values = cache_values.at[micro * P_SIZE:(micro + 1) * P_SIZE].set(fresh_values.reshape(P_SIZE, HW))
            key_heads = cache_keys.reshape(L, HEADS, HD).astype(jnp.float32)
            value_heads = cache_values.reshape(L, HEADS, HD).astype(jnp.float32)
            scores = jnp.einsum('phd,lhd->hpl', queries.astype(jnp.float32), key_heads) * inv_scale
            scores = jnp.where(key_ok[None, None, :], scores, -1e+30)
            peak = lax.optimization_barrier(jnp.max(scores, axis=-1, keepdims=True))
            weights = jnp.where(key_ok[None, None, :], jnp.exp(scores - peak), 0.0)
            total = lax.optimization_barrier(jnp.sum(weights, axis=-1))
            rounded = weights.astype(jnp.bfloat16).astype(jnp.float32)
            mixed = jnp.einsum('hpl,lhd->phd', rounded, value_heads)
            attended = (mixed / jnp.transpose(total)[:, :, None]).reshape(P_SIZE, HW).astype(jnp.bfloat16)
            result = jnp.dot(attended, out_video[block], preferred_element_type=jnp.float32)
            if dual:
                text_result = jnp.dot(attended, out_text[block], preferred_element_type=jnp.float32)
                result = jnp.where(is_text, text_result, result)
            pieces.append((floats + gate_rows * result).astype(jnp.bfloat16))
        hidden = jnp.concatenate(pieces, axis=0)
    return hidden.reshape(N_PIPE, P_SIZE, D)
```

```python
import functools
import math

import jax
import jax.numpy as jnp
from jax import lax
from jax.experimental import pallas as pl
from jax.experimental.pallas import tpu as pltpu
from jax.sharding import PartitionSpec as P

MESH = pl.DeviceIdType.MESH


def unslab(value):
    count, _, half = value.shape
    joined = jnp.concatenate([value[:, :8], value[:, 8:]], axis=2)
    return joined.reshape(count * 8, 2 * half)


def slab(value):
    rows, width = value.shape
    split = value.reshape(rows // 8, 8, width)
    return jnp.concatenate([split[:, :, : width // 2], split[:, :, width // 2 :]], axis=1)


def pipe_kernel(
    sections, dual_count, heads, head_dim,
    bias_ref, hin_ref, mods_ref, gains_ref, wqv_ref, wqt_ref, wov_ref, wot_ref, stale_ref,
    out_ref,
    hid, hnew, obuf, stat_out, stat_in, part_own, part_out, part_in, y_own, y_out, y_in,
    wq, wo, kv,
    init_sem, hid_sem, stat_ssem, stat_rsem, part_ssem, part_rsem, y_ssem, y_rsem,
    next_sem, out_sem, wq_sem, wo_sem, kv_sem,
):
    s = lax.axis_index("pipe")
    i = lax.axis_index("blk")
    j = lax.axis_index("uly")
    me = (s * 2 + i) * 4 + j
    local_width = heads * head_dim
    half = mods_ref.shape[2]
    micro = 64
    inv_scale = 1.0 / math.sqrt(head_dim)
    last = sections - 1

    for c in range(3):
        @pl.when(s < dual_count)
        def _():
            pltpu.make_async_copy(wqt_ref.at[c], wq.at[0, c], wq_sem.at[0, c]).start()

        @pl.when(s >= dual_count)
        def _():
            pltpu.make_async_copy(wqv_ref.at[c], wq.at[0, c], wq_sem.at[0, c]).start()

    @pl.when(s < dual_count)
    def _():
        pltpu.make_async_copy(wot_ref, wo.at[0], wo_sem.at[0]).start()

    @pl.when(s >= dual_count)
    def _():
        pltpu.make_async_copy(wov_ref, wo.at[0], wo_sem.at[0]).start()

    pltpu.make_async_copy(stale_ref, kv, kv_sem.at[0]).start()
    for c in range(3):
        pltpu.make_async_copy(wqv_ref.at[c], wq.at[1, c], wq_sem.at[1, c]).start()
    pltpu.make_async_copy(wov_ref, wo.at[1], wo_sem.at[1]).start()

    barrier = pltpu.get_barrier_semaphore()
    devices = sections * 8

    @pl.loop(0, devices)
    def _(d):
        @pl.when(d != me)
        def _():
            pl.semaphore_signal(
                barrier, inc=1, device_id=(d // 8, (d // 4) % 2, d % 4), device_id_type=MESH
            )

    pl.semaphore_wait(barrier, devices - 1)

    def init_copy(k):
        return pltpu.make_async_remote_copy(
            src_ref=hin_ref.at[k // 4],
            dst_ref=hid.at[s, i * 4 + j],
            send_sem=init_sem.at[k],
            recv_sem=hid_sem.at[s, i * 4 + j],
            device_id=(0, k // 4, k % 4),
            device_id_type=MESH,
        )

    for k in range(8):
        @pl.when(me != k)
        def _():
            init_copy(k).start()

        @pl.when(me == k)
        def _():
            pltpu.make_async_copy(
                hin_ref.at[k // 4], hid.at[s, i * 4 + j], hid_sem.at[s, i * 4 + j]
            ).start()

    def stat_copy(m):
        return pltpu.make_async_remote_copy(
            src_ref=stat_out.at[m], dst_ref=stat_in.at[m],
            send_sem=stat_ssem.at[m], recv_sem=stat_rsem.at[m],
            device_id=(s, 1 - i, j), device_id_type=MESH,
        )

    def part_copy(m, c):
        return pltpu.make_async_remote_copy(
            src_ref=part_out.at[m, c], dst_ref=part_in.at[m, c],
            send_sem=part_ssem.at[m, c], recv_sem=part_rsem.at[m, c],
            device_id=(s, 1 - i, j), device_id_type=MESH,
        )

    def y_copy(m, o):
        to = (j + o) % 4
        return pltpu.make_async_remote_copy(
            src_ref=y_out.at[m, to], dst_ref=y_in.at[m, o - 1],
            send_sem=y_ssem.at[m, o - 1], recv_sem=y_rsem.at[m, o - 1],
            device_id=(s, i, to), device_id_type=MESH,
        )

    def next_copy(m, to):
        return pltpu.make_async_remote_copy(
            src_ref=hnew.at[m], dst_ref=hid.at[m, pl.ds(2 * j, 2)],
            send_sem=next_sem.at[m, to], recv_sem=hid_sem.at[m, j],
            device_id=(s + 1, i, to), device_id_type=MESH,
        )

    def out_copy(m, e):
        g = 2 * j + e
        return pltpu.make_async_remote_copy(
            src_ref=hnew.at[m, e], dst_ref=obuf.at[i],
            send_sem=next_sem.at[m, e], recv_sem=out_sem.at[i],
            device_id=(m, g // 4, g % 4), device_id_type=MESH,
        )

    def owner(m, e):
        return m * 8 + 2 * j + e

    def stage_a(m):
        @pl.when(s == 0)
        def _():
            for r in range(8):
                pltpu.make_async_copy(hid.at[m, r], hid.at[m, r], hid_sem.at[m, r]).wait()

        @pl.when(s > 0)
        def _():
            for r in range(4):
                pair = hid.at[m, pl.ds(2 * r, 2)]
                pltpu.make_async_copy(pair, pair, hid_sem.at[m, r]).wait()

        floats = unslab(hid[m].astype(jnp.float32))
        mean = jnp.mean(floats, axis=-1, keepdims=True)
        centred = floats - mean
        spread = jnp.sum(centred * centred, axis=-1, keepdims=True)
        lanes = lax.broadcasted_iota(jnp.int32, (micro, 128), 1)
        stat_out[m] = jnp.where(lanes < 64, mean, spread)
        stat_copy(m).start()

    def stage_b(m, sel):
        floats = unslab(hid[m].astype(jnp.float32))
        stat_copy(m).wait_recv()
        mean_a, spread_a = stat_out[m, :, 0:1], stat_out[m, :, 64:65]
        mean_b, spread_b = stat_in[m, :, 0:1], stat_in[m, :, 64:65]
        mean = 0.5 * (mean_a + mean_b)
        delta = mean_a - mean_b
        var = (spread_a + spread_b + delta * delta * (0.5 * half)) / (2 * half)
        scale = 1.0 + mods_ref[sel, 1:2, :]
        shift = mods_ref[sel, 0:1, :]
        normed = (floats - mean) * lax.rsqrt(var + 1e-06)
        modded = (normed * scale + shift).astype(jnp.bfloat16)
        for c in range(3):
            @pl.when(m < 2)
            def _():
                pltpu.make_async_copy(wqv_ref.at[c], wq.at[m % 2, c], wq_sem.at[m % 2, c]).wait()

            part = jnp.dot(modded, wq[sel, c], preferred_element_type=jnp.float32)
            part_own[c] = part
            part_out[m, c] = part.astype(jnp.bfloat16)
            part_copy(m, c).start()

    def stage_c(m, sel):
        def take(c):
            part_copy(m, c).wait_recv()
            return part_own[c] + part_in[m, c].astype(jnp.float32)

        def norm(value, gain):
            pieces = []
            for h in range(heads):
                one = value[:, h * head_dim : (h + 1) * head_dim]
                squares = jnp.mean(one * one, axis=-1, keepdims=True)
                pieces.append((one * lax.rsqrt(squares + 1e-06) * gain).astype(jnp.bfloat16))
            return pieces

        @pl.when(m == 0)
        def _():
            pltpu.make_async_copy(stale_ref, kv, kv_sem.at[0]).wait()

        @pl.when(m < 2)
        def _():
            pltpu.make_async_copy(wov_ref, wo.at[m % 2], wo_sem.at[m % 2]).wait()

        queries = norm(take(0), gains_ref[sel, 0:1, :])
        kv[0, m] = jnp.concatenate(norm(take(1), gains_ref[sel, 1:2, :]), axis=1)
        kv[1, m] = take(2).astype(jnp.bfloat16)
        bias = bias_ref[0:1, :]
        outs = []
        for h in range(heads):
            cols = slice(h * head_dim, (h + 1) * head_dim)
            keys = kv[0, :, :, cols].reshape(sections * micro, head_dim)
            values = kv[1, :, :, cols].reshape(sections * micro, head_dim)
            scores = lax.dot_general(
                queries[h], keys, (((1,), (1,)), ((), ())), preferred_element_type=jnp.float32
            )
            scores = scores * inv_scale + bias
            peak = jnp.max(scores, axis=-1, keepdims=True)
            weights = jnp.exp(scores - peak)
            total = jnp.sum(weights, axis=-1, keepdims=True)
            mixed = jnp.dot(
                weights.astype(jnp.bfloat16), values, preferred_element_type=jnp.float32
            )
            outs.append((mixed / total).astype(jnp.bfloat16))
        attended = jnp.concatenate(outs, axis=1)
        y = jnp.dot(attended, wo[sel], preferred_element_type=jnp.float32)
        y = y.reshape(4, micro // 4, half)
        y_own[...] = y
        y_out[m] = y.astype(jnp.bfloat16)
        for o in (2, 3, 1):
            y_copy(m, o).start()

    def stage_d(m, sel):
        total = y_own[j]
        for o in (1, 2, 3):
            y_copy(m, o).wait_recv()
            total = total + y_in[m, o - 1].astype(jnp.float32)
        old = unslab(hid[m, pl.ds(2 * j, 2)].astype(jnp.float32))
        new = old + mods_ref[sel, 2:3, :] * total
        hnew[m] = slab(new).astype(jnp.bfloat16)

        @pl.when(s < last)
        def _():
            for to in range(4):
                next_copy(m, to).start()

        @pl.when(s == last)
        def _():
            for e in range(2):
                @pl.when(me != owner(m, e))
                def _():
                    out_copy(m, e).start()

                @pl.when(me == owner(m, e))
                def _():
                    pltpu.make_async_copy(hnew.at[m, e], obuf.at[i], out_sem.at[i]).start()

    stage_a(0)

    @pl.loop(0, sections)
    def _(m):
        sel = jnp.minimum(m, 1)
        stage_b(m, sel)
        stage_c(m, sel)

        @pl.when(m < last)
        def _():
            stage_a(m + 1)

        stage_d(m, sel)

    for k in range(8):
        @pl.when(me != k)
        def _():
            init_copy(k).wait_send()

    @pl.loop(0, sections)
    def _(m):
        stat_copy(m).wait_send()
        for c in range(3):
            part_copy(m, c).wait_send()
        for o in (1, 2, 3):
            y_copy(m, o).wait_send()

        @pl.when(s < last)
        def _():
            for to in range(4):
                next_copy(m, to).wait_send()

        @pl.when(s == last)
        def _():
            for e in range(2):
                @pl.when(me != owner(m, e))
                def _():
                    out_copy(m, e).wait_send()

    for side in range(2):
        pltpu.make_async_copy(obuf.at[side], obuf.at[side], out_sem.at[side]).wait()
    out_ref[...] = obuf[...]


def fused(
    hidden_in, text_len, qkv_video, qkv_text, out_video, out_text, modulation, qk_gain, stale_kv
):
    sections = lax.axis_size("pipe")
    section = lax.axis_index("pipe")
    blk_index = lax.axis_index("blk")
    rows, width = hidden_in.shape[1:]
    half = width // 2
    micro = rows * 8
    dual_count = qkv_text.shape[0]
    head_dim = qk_gain.shape[3]
    local_width = stale_kv.shape[3]
    heads = local_width // head_dim
    dual = section < dual_count
    chosen = jnp.minimum(section, dual_count - 1)
    wqv = jnp.transpose(qkv_video[0], (1, 0, 2))
    wqt = jnp.transpose(
        lax.dynamic_index_in_dim(qkv_text, chosen, 0, keepdims=False), (1, 0, 2)
    )
    wot = lax.dynamic_index_in_dim(out_text, chosen, 0, keepdims=False)
    mine = lax.dynamic_slice_in_dim(modulation[0], blk_index * half, half, 2)
    mods = jnp.stack([jnp.where(dual, mine[1], mine[0]), mine[0]])
    gains = qk_gain[0]
    gains = jnp.stack([jnp.where(dual, gains[1], gains[0]), gains[0]])
    places = jnp.arange(micro * sections, dtype=jnp.int32)
    key_ok = (places >= micro) | (places < text_len[0])
    bias = jnp.broadcast_to(jnp.where(key_ok, 0.0, -1e30).astype(jnp.float32), (8, places.size))
    stale = stale_kv[0].reshape(2, sections, micro, local_width)
    quarter = half // 2
    hin = hidden_in[0].reshape(rows, 2, 2, quarter)
    hin = jnp.transpose(hin, (1, 2, 0, 3)).reshape(2, 2 * rows, quarter)
    bf16, f32 = jnp.bfloat16, jnp.float32
    dma = pltpu.SemaphoreType.DMA
    vmem = pl.BlockSpec(memory_space=pltpu.VMEM)
    anyspace = pl.BlockSpec(memory_space=pl.ANY)
    out = pl.pallas_call(
        functools.partial(pipe_kernel, sections, dual_count, heads, head_dim),
        out_shape=jax.ShapeDtypeStruct((2, 2 * rows, quarter), bf16),
        in_specs=[vmem] * 4 + [anyspace] * 5,
        out_specs=vmem,
        scratch_shapes=[
            pltpu.VMEM((sections, 8, 2 * rows, quarter), bf16),
            pltpu.VMEM((sections, 2, 2 * rows, quarter), bf16),
            pltpu.VMEM((2, 2 * rows, quarter), bf16),
            pltpu.VMEM((sections, micro, 128), f32),
            pltpu.VMEM((sections, micro, 128), f32),
            pltpu.VMEM((3, micro, local_width), f32),
            pltpu.VMEM((sections, 3, micro, local_width), bf16),
            pltpu.VMEM((sections, 3, micro, local_width), bf16),
            pltpu.VMEM((4, micro // 4, half), f32),
            pltpu.VMEM((sections, 4, micro // 4, half), bf16),
            pltpu.VMEM((sections, 3, micro // 4, half), bf16),
            pltpu.VMEM((2, 3, half, local_width), bf16),
            pltpu.VMEM((2, local_width, half), bf16),
            pltpu.VMEM((2, sections, micro, local_width), bf16),
            dma((8,)),
            dma((sections, 8)),
            dma((sections,)),
            dma((sections,)),
            dma((sections, 3)),
            dma((sections, 3)),
            dma((sections, 3)),
            dma((sections, 3)),
            dma((sections, 4)),
            dma((2,)),
            dma((2, 3)),
            dma((2,)),
            dma((1,)),
        ],
        compiler_params=pltpu.CompilerParams(
            collective_id=0, has_side_effects=True, vmem_limit_bytes=40 * 1024 * 1024
        ),
        cost_estimate=pl.CostEstimate(
            flops=8 * micro * sections * half * local_width,
            bytes_accessed=16 * half * local_width,
            transcendentals=heads * micro * sections * micro * sections,
        ),
    )(bias, hin, mods, gains, wqv, wqt, out_video[0], wot, stale)
    out = out.reshape(2, 2, rows, quarter)
    return jnp.transpose(out, (2, 0, 1, 3)).reshape(1, rows, width)


def from_behind(shard, axis, by):
    size = lax.axis_size(axis)
    pairs = [(i, i + by) for i in range(size) if 0 <= i + by < size]
    return lax.ppermute(shard, axis, pairs)


def rms_scale(values, gain):
    squares = jnp.mean(values * values, axis=-1, keepdims=True)
    return values * lax.rsqrt(squares + 1e-06) * gain


def local(
    hidden_in, text_len, qkv_video, qkv_text, out_video, out_text, modulation, qk_gain, stale_kv
):
    sections = lax.axis_size("pipe")
    blk_count = lax.axis_size("blk")
    uly_count = lax.axis_size("uly")
    section = lax.axis_index("pipe")
    blk_index = lax.axis_index("blk")
    rows = hidden_in.shape[1]
    width = hidden_in.shape[2]
    group = rows * uly_count
    micro = group * blk_count
    text_count = 2 * group
    dual_count = qkv_text.shape[0]
    head_dim = qk_gain.shape[3]
    local_width = stale_kv.shape[3]
    local_heads = local_width // head_dim
    inv_scale = 1.0 / math.sqrt(head_dim)
    dual = section < dual_count
    chosen = jnp.minimum(section, dual_count - 1)
    text_rows_w = lax.dynamic_index_in_dim(qkv_text, chosen, 0, keepdims=False)
    text_cols_w = lax.dynamic_index_in_dim(out_text, chosen, 0, keepdims=False)
    video_proj, text_proj, video_back, text_back = (
        lax.all_gather(qkv_video[0], "blk", axis=0, tiled=True),
        lax.all_gather(text_rows_w, "blk", axis=0, tiled=True),
        lax.all_gather(out_video[0], "blk", axis=1, tiled=True),
        lax.all_gather(text_cols_w, "blk", axis=1, tiled=True),
    )
    video_proj = video_proj.reshape(width, 3 * local_width)
    text_proj = text_proj.reshape(width, 3 * local_width)
    mods = modulation[0]
    gains = qk_gain[0]
    stale = stale_kv[0]
    valid_text = text_len[0]
    cache_keys = stale[0]
    cache_values = stale[1]
    places = jnp.arange(micro * sections, dtype=jnp.int32)
    key_ok = (places >= text_count) | (places < valid_text)
    carried = jnp.zeros((rows, width), jnp.bfloat16)
    inbox = hidden_in[0]
    outbox = jnp.zeros((rows, width), jnp.bfloat16)
    last_tick = 2 * sections - 2
    for tick in range(2 * sections - 1):
        micro_index = tick - section
        valid = (micro_index >= 0) & (micro_index < sections)
        current = jnp.clip(micro_index, 0, sections - 1)
        entering = jnp.where(section == 0, inbox, carried)
        is_text = dual & (current * micro + blk_index * group < text_count)
        stream = is_text.astype(jnp.int32)
        mod_rows = lax.dynamic_index_in_dim(mods, stream, 0, keepdims=False)
        gain_rows = lax.dynamic_index_in_dim(gains, stream, 0, keepdims=False)
        floats = entering.astype(jnp.float32)
        centred = floats - jnp.mean(floats, axis=-1, keepdims=True)
        normed = centred * lax.rsqrt(jnp.mean(centred * centred, axis=-1, keepdims=True) + 1e-06)
        modded = (normed * (1.0 + mod_rows[1]) + mod_rows[0]).astype(jnp.bfloat16)
        gathered = lax.all_gather(modded, "uly", axis=0, tiled=True)
        projected = lax.cond(
            is_text,
            lambda operand: jnp.dot(operand, text_proj, preferred_element_type=jnp.float32),
            lambda operand: jnp.dot(operand, video_proj, preferred_element_type=jnp.float32),
            gathered,
        )
        projected = projected.reshape(group, 3, local_heads, head_dim)
        queries = rms_scale(projected[:, 0], gain_rows[0]).astype(jnp.bfloat16)
        fresh_keys = (
            rms_scale(projected[:, 1], gain_rows[1])
            .astype(jnp.bfloat16)
            .reshape(group, local_width)
        )
        fresh_values = projected[:, 2].astype(jnp.bfloat16).reshape(group, local_width)
        all_keys, all_values = (
            lax.all_gather(fresh_keys, "blk", axis=0, tiled=True),
            lax.all_gather(fresh_values, "blk", axis=0, tiled=True),
        )
        offset = current * micro
        old_keys = lax.dynamic_slice_in_dim(cache_keys, offset, micro, 0)
        old_values = lax.dynamic_slice_in_dim(cache_values, offset, micro, 0)
        cache_keys = lax.dynamic_update_slice_in_dim(
            cache_keys, jnp.where(valid, all_keys, old_keys), offset, 0
        )
        cache_values = lax.dynamic_update_slice_in_dim(
            cache_values, jnp.where(valid, all_values, old_values), offset, 0
        )
        key_heads = cache_keys.reshape(-1, local_heads, head_dim)
        value_heads = cache_values.reshape(-1, local_heads, head_dim)
        scores = (
            jnp.einsum("rhd,lhd->hrl", queries, key_heads, preferred_element_type=jnp.float32)
            * inv_scale
        )
        scores = jnp.where(key_ok[None, None, :], scores, -1e30)
        peak = jnp.max(scores, axis=-1, keepdims=True)
        weights = jnp.where(key_ok[None, None, :], jnp.exp(scores - peak), 0.0)
        total = jnp.sum(weights, axis=-1)
        mixed = jnp.einsum(
            "hrl,lhd->rhd",
            weights.astype(jnp.bfloat16),
            value_heads,
            preferred_element_type=jnp.float32,
        )
        attended = (
            (mixed / jnp.transpose(total)[:, :, None])
            .reshape(group, local_width)
            .astype(jnp.bfloat16)
        )
        partial_value = lax.cond(
            is_text,
            lambda operand: jnp.dot(operand, text_back, preferred_element_type=jnp.float32),
            lambda operand: jnp.dot(operand, video_back, preferred_element_type=jnp.float32),
            attended,
        )
        summed = lax.psum_scatter(partial_value, "uly", scatter_dimension=0, tiled=True)
        leaving = (floats + mod_rows[2] * summed).astype(jnp.bfloat16)
        outbox = jnp.where((section == sections - 1) & valid, leaving, outbox)
        if tick < last_tick:
            carried = from_behind(leaving, "pipe", 1)
            inbox, outbox = from_behind((inbox, outbox), "pipe", -1)
    return outbox[None]


def solution(mesh):
    shape = mesh.shape
    small = shape["blk"] == 2 and shape["uly"] == 4 and shape["pipe"] == 4
    return jax.shard_map(
        fused if small else local,
        mesh=mesh,
        in_specs=(
            P("pipe", ("blk", "uly"), None),
            P(),
            P("pipe", "blk", None, "uly"),
            P(None, "blk", None, "uly"),
            P("pipe", "uly", "blk"),
            P(None, "uly", "blk"),
            P("pipe", None, None, None),
            P("pipe", None, None, None),
            P("pipe", None, None, "uly"),
        ),
        out_specs=P("pipe", ("blk", "uly"), None),
        check_vma=False,
    )
```

```python
import functools
import math

import jax
import jax.numpy as jnp
from jax import lax
from jax.experimental import pallas as pl
from jax.experimental.pallas import tpu as pltpu
from jax.sharding import PartitionSpec as P

MESH = pl.DeviceIdType.MESH


def unslab(value):
    count, _, half = value.shape
    joined = jnp.concatenate([value[:, :8], value[:, 8:]], axis=2)
    return joined.reshape(count * 8, 2 * half)


def slab(value):
    rows, width = value.shape
    split = value.reshape(rows // 8, 8, width)
    return jnp.concatenate([split[:, :, : width // 2], split[:, :, width // 2 :]], axis=1)


def pipe_kernel(
    sections, dual_count, heads, head_dim,
    len_ref, hin_ref, mod_ref, gain_ref, wqv_ref, wqt_ref, wov_ref, wot_ref, stale_ref,
    out_ref,
    mods, gains, hid, hnew, obuf, stat_first, stat_out, stat_in, part_own, part_out, part_in, y_own, y_out, y_in,
    wq, wo, kv,
    init_sem, hid_sem, fwd_sem, first_sem, stat_ssem, stat_rsem, part_ssem, part_rsem, y_ssem, y_rsem,
    next_sem, out_sem, wq_sem, wo_sem, kv_sem,
):
    s = lax.axis_index("pipe")
    i = lax.axis_index("blk")
    j = lax.axis_index("uly")
    me = (s * 2 + i) * 4 + j
    local_width = heads * head_dim
    half = mods.shape[2]
    micro = 64
    inv_scale = 1.0 / math.sqrt(head_dim)
    last = sections - 1

    chosen = jnp.minimum(s, dual_count - 1)
    edges = list(range(0, 3 * local_width, 256)) + [3 * local_width]
    chunks = list(zip(edges[:-1], edges[1:]))

    def weight_copy(source, slot, c):
        return pltpu.make_async_copy(
            source, wq.at[slot, :, pl.ds(c * local_width, local_width)], wq_sem.at[slot, c]
        )

    for c in range(3):
        @pl.when(s < dual_count)
        def _():
            weight_copy(wqt_ref.at[chosen, c], 0, c).start()

        @pl.when(s >= dual_count)
        def _():
            weight_copy(wqv_ref.at[c], 0, c).start()

    @pl.when(s < dual_count)
    def _():
        pltpu.make_async_copy(wot_ref.at[chosen], wo.at[0], wo_sem.at[0]).start()

    @pl.when(s >= dual_count)
    def _():
        pltpu.make_async_copy(wov_ref, wo.at[0], wo_sem.at[0]).start()

    pltpu.make_async_copy(stale_ref, kv, kv_sem.at[0]).start()
    for c in range(3):
        weight_copy(wqv_ref.at[c], 1, c).start()
    pltpu.make_async_copy(wov_ref, wo.at[1], wo_sem.at[1]).start()

    barrier = pltpu.get_barrier_semaphore()
    devices = sections * 8

    @pl.loop(0, devices)
    def _(d):
        @pl.when(d != me)
        def _():
            pl.semaphore_signal(
                barrier, inc=1, device_id=(d // 8, (d // 4) % 2, d % 4), device_id_type=MESH
            )

    dual = s < dual_count
    cols = pl.ds(pl.multiple_of(i * half, 128), half)
    for k in range(3):
        video, text = mod_ref[k, 0:1, cols], mod_ref[k, 1:2, cols]
        mods[0, k : k + 1, :] = jnp.where(dual, text, video)
        mods[1, k : k + 1, :] = video
    gains[1] = gain_ref[0]
    gains[0] = jnp.where(dual, gain_ref[1], gain_ref[0])

    def stats_of(floats):
        mean = jnp.mean(floats, axis=-1, keepdims=True)
        centred = floats - mean
        spread = jnp.sum(centred * centred, axis=-1, keepdims=True)
        return mean, spread

    def packed_stats(floats):
        mean, spread = stats_of(floats)
        lanes = lax.broadcasted_iota(jnp.int32, (floats.shape[0], 128), 1)
        return jnp.where(lanes < 64, mean, spread).reshape(-1, 8, 128)

    for side in range(2):
        stat_first[side] = packed_stats(unslab(hin_ref[side : side + 1].astype(jnp.float32)))[0]

    pl.semaphore_wait(barrier, devices - 1)

    def init_copy(k):
        return pltpu.make_async_remote_copy(
            src_ref=hin_ref.at[k // 4],
            dst_ref=hid.at[s, i * 4 + j],
            send_sem=init_sem.at[k],
            recv_sem=hid_sem.at[s, i * 4 + j],
            device_id=(0, k // 4, k % 4),
            device_id_type=MESH,
        )

    def first_copy(k):
        return pltpu.make_async_remote_copy(
            src_ref=stat_first.at[1 - k // 4],
            dst_ref=stat_in.at[s, i * 4 + j],
            send_sem=first_sem.at[k],
            recv_sem=stat_rsem.at[s, i * 4 + j],
            device_id=(0, k // 4, k % 4),
            device_id_type=MESH,
        )

    for k in range(8):
        @pl.when(me != k)
        def _():
            init_copy(k).start()
            first_copy(k).start()

        @pl.when(me == k)
        def _():
            pltpu.make_async_copy(
                hin_ref.at[k // 4], hid.at[s, i * 4 + j], hid_sem.at[s, i * 4 + j]
            ).start()
            pltpu.make_async_copy(
                stat_first.at[1 - k // 4], stat_in.at[s, i * 4 + j], stat_rsem.at[s, i * 4 + j]
            ).start()

    def stat_copy(m, to):
        return pltpu.make_async_remote_copy(
            src_ref=stat_out.at[m], dst_ref=stat_in.at[m, pl.ds(2 * j, 2)],
            send_sem=stat_ssem.at[m, to], recv_sem=stat_rsem.at[m, j],
            device_id=(s + 1, 1 - i, to), device_id_type=MESH,
        )

    def part_copy(m, c):
        return pltpu.make_async_remote_copy(
            src_ref=part_out.at[m, :, pl.ds(chunks[c][0], chunks[c][1] - chunks[c][0])],
            dst_ref=part_in.at[m, :, pl.ds(chunks[c][0], chunks[c][1] - chunks[c][0])],
            send_sem=part_ssem.at[m, c], recv_sem=part_rsem.at[m, c],
            device_id=(s, 1 - i, j), device_id_type=MESH,
        )

    def y_copy(m, o, e):
        to = (j + o) % 4
        slot = 2 * (o - 1) + e
        return pltpu.make_async_remote_copy(
            src_ref=y_out.at[m, 2 * to + e], dst_ref=y_in.at[m, slot],
            send_sem=y_ssem.at[m, slot], recv_sem=y_rsem.at[m, slot],
            device_id=(s, i, to), device_id_type=MESH,
        )

    parity = j % 2

    def next_copy(m, e, side):
        return pltpu.make_async_remote_copy(
            src_ref=hnew.at[m, e], dst_ref=hid.at[m, 2 * j + e],
            send_sem=next_sem.at[m, 2 * e + side], recv_sem=hid_sem.at[m, 2 * j + e],
            device_id=(s + 1, i, 2 * side + parity), device_id_type=MESH,
        )

    def forward_copy(m, e, side):
        g = 2 * (2 * side + parity) + e
        return pltpu.make_async_remote_copy(
            src_ref=hid.at[m, g], dst_ref=hid.at[m, g],
            send_sem=fwd_sem.at[m, 2 * e + side], recv_sem=hid_sem.at[m, g],
            device_id=(s, i, j + 1 - 2 * parity), device_id_type=MESH,
        )

    def out_copy(m, e):
        g = 2 * j + e
        return pltpu.make_async_remote_copy(
            src_ref=hnew.at[m, e], dst_ref=obuf.at[i],
            send_sem=next_sem.at[m, e], recv_sem=out_sem.at[i],
            device_id=(m, g // 4, g % 4), device_id_type=MESH,
        )

    def owner(m, e):
        return m * 8 + 2 * j + e

    def arrive(m):
        def take(ref, sem):
            pltpu.make_async_copy(ref, ref, sem).wait()

        @pl.when(s == 0)
        def _():
            for r in range(8):
                take(hid.at[m, r], hid_sem.at[m, r])
                take(stat_in.at[m, r], stat_rsem.at[m, r])

        @pl.when(s > 0)
        def _():
            for e in range(2):
                for side in range(2):
                    g = 2 * (2 * side + parity) + e
                    take(hid.at[m, g], hid_sem.at[m, g])
                    forward_copy(m, e, side).start()
            for e in range(2):
                for side in range(2):
                    g = 2 * (2 * side + 1 - parity) + e
                    take(hid.at[m, g], hid_sem.at[m, g])
            for r in range(4):
                take(stat_in.at[m, pl.ds(2 * r, 2)], stat_rsem.at[m, r])

    def stage_b(m, sel):
        arrive(m)
        floats = unslab(hid[m].astype(jnp.float32))
        mean_a, spread_a = stats_of(floats)
        other = stat_in[m].reshape(micro, 128)
        mean_b, spread_b = other[:, 0:1], other[:, 64:65]
        mean = 0.5 * (mean_a + mean_b)
        delta = mean_a - mean_b
        var = (spread_a + spread_b + delta * delta * (0.5 * half)) / (2 * half)
        scale = 1.0 + mods[sel, 1:2, :]
        shift = mods[sel, 0:1, :]
        normed = (floats - mean) * lax.rsqrt(var + 1e-06)
        modded = (normed * scale + shift).astype(jnp.bfloat16)

        @pl.when(m < 2)
        def _():
            for c in range(3):
                weight_copy(wqv_ref.at[c], sel, c).wait()

        for c, (lo, hi) in enumerate(chunks):
            part = jnp.dot(modded, wq[sel, :, lo:hi], preferred_element_type=jnp.float32)
            part_own[m % 2, :, lo:hi] = part
            part_out[m, :, lo:hi] = part.astype(jnp.bfloat16)
            part_copy(m, c).start()

    def stage_c(m, sel):
        early = [c for c in range(len(chunks)) if chunks[c][0] < 2 * local_width]
        for c in early:
            part_copy(m, c).wait_recv()

        def take(c):
            lo, hi = c * local_width, (c + 1) * local_width
            return part_own[m % 2, :, lo:hi] + part_in[m, :, lo:hi].astype(jnp.float32)

        def norm(value, gain):
            pieces = []
            for h in range(heads):
                one = value[:, h * head_dim : (h + 1) * head_dim]
                squares = jnp.mean(one * one, axis=-1, keepdims=True)
                pieces.append((one * lax.rsqrt(squares + 1e-06) * gain).astype(jnp.bfloat16))
            return pieces

        @pl.when(m == 0)
        def _():
            pltpu.make_async_copy(stale_ref, kv, kv_sem.at[0]).wait()

        @pl.when(m < 2)
        def _():
            pltpu.make_async_copy(wov_ref, wo.at[sel], wo_sem.at[sel]).wait()

        queries = norm(take(0), gains[sel, 0:1, :])
        kv[0, m] = jnp.concatenate(norm(take(1), gains[sel, 1:2, :]), axis=1)
        places = lax.broadcasted_iota(jnp.int32, (1, sections * micro), 1)
        bias = jnp.where((places >= micro) | (places < len_ref[0]), 0.0, -1e30)
        raised = []
        for h in range(heads):
            cols = slice(h * head_dim, (h + 1) * head_dim)
            keys = kv[0, :, :, cols].reshape(sections * micro, head_dim)
            scores = lax.dot_general(
                queries[h], keys, (((1,), (1,)), ((), ())), preferred_element_type=jnp.float32
            )
            scores = scores * inv_scale + bias
            peak = jnp.max(scores, axis=-1, keepdims=True)
            weights = jnp.exp(scores - peak)
            total = jnp.sum(weights, axis=-1, keepdims=True)
            raised.append((weights.astype(jnp.bfloat16), total))
        for c in range(len(early), len(chunks)):
            part_copy(m, c).wait_recv()
        kv[1, m] = take(2).astype(jnp.bfloat16)
        outs = []
        for h, (weights, total) in enumerate(raised):
            cols = slice(h * head_dim, (h + 1) * head_dim)
            values = kv[1, :, :, cols].reshape(sections * micro, head_dim)
            mixed = jnp.dot(weights, values, preferred_element_type=jnp.float32)
            outs.append((mixed / total).astype(jnp.bfloat16))
        attended = jnp.concatenate(outs, axis=1)
        y = slab(jnp.dot(attended, wo[sel], preferred_element_type=jnp.float32))
        y_own[...] = y
        y_out[m] = y.astype(jnp.bfloat16)
        for e in range(2):
            for o in (2, 3, 1):
                y_copy(m, o, e).start()

    def stage_d(m, sel):
        gate = mods[sel, 2:3, :]
        gate = slab(jnp.broadcast_to(gate, (8, half)))[0]
        for e in range(2):
            total = y_own[2 * j + e]
            for o in (1, 2, 3):
                y_copy(m, o, e).wait_recv()
                total = total + y_in[m, 2 * (o - 1) + e].astype(jnp.float32)
            old = hid[m, 2 * j + e].astype(jnp.float32)
            hnew[m, e] = (old + gate * total).astype(jnp.bfloat16)

            @pl.when(s < last)
            def _():
                for side in range(2):
                    next_copy(m, e, side).start()

            @pl.when(s == last)
            def _():
                @pl.when(me != owner(m, e))
                def _():
                    out_copy(m, e).start()

                @pl.when(me == owner(m, e))
                def _():
                    pltpu.make_async_copy(hnew.at[m, e], obuf.at[i], out_sem.at[i]).start()

        @pl.when(s < last)
        def _():
            stat_out[m] = packed_stats(unslab(hnew[m].astype(jnp.float32)))
            for to in range(4):
                stat_copy(m, to).start()

    stage_b(0, 0)

    @pl.loop(0, sections)
    def _(m):
        sel = jnp.minimum(m, 1)
        stage_c(m, sel)

        @pl.when(m < last)
        def _():
            stage_b(m + 1, 1)

        stage_d(m, sel)

    for k in range(8):
        @pl.when(me != k)
        def _():
            init_copy(k).wait_send()
            first_copy(k).wait_send()

    @pl.loop(0, sections)
    def _(m):
        for c in range(len(chunks)):
            part_copy(m, c).wait_send()
        for e in range(2):
            for o in (1, 2, 3):
                y_copy(m, o, e).wait_send()

        @pl.when(s > 0)
        def _():
            for e in range(2):
                for side in range(2):
                    forward_copy(m, e, side).wait_send()

        @pl.when(s < last)
        def _():
            for e in range(2):
                for side in range(2):
                    next_copy(m, e, side).wait_send()
            for to in range(4):
                stat_copy(m, to).wait_send()

        @pl.when(s == last)
        def _():
            for e in range(2):
                @pl.when(me != owner(m, e))
                def _():
                    out_copy(m, e).wait_send()

    for side in range(2):
        pltpu.make_async_copy(obuf.at[side], obuf.at[side], out_sem.at[side]).wait()
    out_ref[...] = obuf[...]


def fused(
    hidden_in, text_len, qkv_video, qkv_text, out_video, out_text, modulation, qk_gain, stale_kv
):
    sections = lax.axis_size("pipe")
    rows, width = hidden_in.shape[1:]
    half = width // 2
    micro = rows * 8
    dual_count = qkv_text.shape[0]
    head_dim = qk_gain.shape[3]
    local_width = stale_kv.shape[3]
    heads = local_width // head_dim
    wqv = jnp.transpose(qkv_video[0], (1, 0, 2))
    wqt = jnp.transpose(qkv_text, (0, 2, 1, 3))
    mods = jnp.transpose(modulation[0], (1, 0, 2))
    stale = stale_kv[0].reshape(2, sections, micro, local_width)
    quarter = half // 2
    hin = hidden_in[0].reshape(rows, 2, 2, quarter)
    hin = jnp.transpose(hin, (1, 2, 0, 3)).reshape(2, 2 * rows, quarter)
    pieces = -(-3 * local_width // 256)
    bf16, f32 = jnp.bfloat16, jnp.float32
    dma = pltpu.SemaphoreType.DMA
    vmem = pl.BlockSpec(memory_space=pltpu.VMEM)
    anyspace = pl.BlockSpec(memory_space=pl.ANY)
    out = pl.pallas_call(
        functools.partial(pipe_kernel, sections, dual_count, heads, head_dim),
        out_shape=jax.ShapeDtypeStruct((2, 2 * rows, quarter), bf16),
        in_specs=[pl.BlockSpec(memory_space=pltpu.SMEM)] + [vmem] * 3 + [anyspace] * 5,
        out_specs=vmem,
        scratch_shapes=[
            pltpu.VMEM((2, 3, half), f32),
            pltpu.VMEM((2, 2, head_dim), f32),
            pltpu.VMEM((sections, 8, 2 * rows, quarter), bf16),
            pltpu.VMEM((sections, 2, 2 * rows, quarter), bf16),
            pltpu.VMEM((2, 2 * rows, quarter), bf16),
            pltpu.VMEM((2, 8, 128), f32),
            pltpu.VMEM((sections, 2, 8, 128), f32),
            pltpu.VMEM((sections, 8, 8, 128), f32),
            pltpu.VMEM((2, micro, 3 * local_width), f32),
            pltpu.VMEM((sections, micro, 3 * local_width), bf16),
            pltpu.VMEM((sections, micro, 3 * local_width), bf16),
            pltpu.VMEM((8, 2 * rows, quarter), f32),
            pltpu.VMEM((sections, 8, 2 * rows, quarter), bf16),
            pltpu.VMEM((sections, 6, 2 * rows, quarter), bf16),
            pltpu.VMEM((2, half, 3 * local_width), bf16),
            pltpu.VMEM((2, local_width, half), bf16),
            pltpu.VMEM((2, sections, micro, local_width), bf16),
            dma((8,)),
            dma((sections, 8)),
            dma((sections, 4)),
            dma((8,)),
            dma((sections, 4)),
            dma((sections, 8)),
            dma((sections, pieces)),
            dma((sections, pieces)),
            dma((sections, 6)),
            dma((sections, 6)),
            dma((sections, 4)),
            dma((2,)),
            dma((2, 3)),
            dma((2,)),
            dma((1,)),
        ],
        compiler_params=pltpu.CompilerParams(
            collective_id=0, has_side_effects=True, vmem_limit_bytes=60 * 1024 * 1024
        ),
        cost_estimate=pl.CostEstimate(
            flops=8 * micro * sections * half * local_width,
            bytes_accessed=16 * half * local_width,
            transcendentals=heads * micro * sections * micro * sections,
        ),
    )(text_len, hin, mods, qk_gain[0], wqv, wqt, out_video[0], out_text, stale)
    out = out.reshape(2, 2, rows, quarter)
    return jnp.transpose(out, (2, 0, 1, 3)).reshape(1, rows, width)


def from_behind(shard, axis, by):
    size = lax.axis_size(axis)
    pairs = [(i, i + by) for i in range(size) if 0 <= i + by < size]
    return lax.ppermute(shard, axis, pairs)


def rms_scale(values, gain):
    squares = jnp.mean(values * values, axis=-1, keepdims=True)
    return values * lax.rsqrt(squares + 1e-06) * gain


def local(
    hidden_in, text_len, qkv_video, qkv_text, out_video, out_text, modulation, qk_gain, stale_kv
):
    sections = lax.axis_size("pipe")
    blk_count = lax.axis_size("blk")
    uly_count = lax.axis_size("uly")
    section = lax.axis_index("pipe")
    blk_index = lax.axis_index("blk")
    rows = hidden_in.shape[1]
    width = hidden_in.shape[2]
    group = rows * uly_count
    micro = group * blk_count
    text_count = 2 * group
    dual_count = qkv_text.shape[0]
    head_dim = qk_gain.shape[3]
    local_width = stale_kv.shape[3]
    local_heads = local_width // head_dim
    inv_scale = 1.0 / math.sqrt(head_dim)
    dual = section < dual_count
    chosen = jnp.minimum(section, dual_count - 1)
    text_rows_w = lax.dynamic_index_in_dim(qkv_text, chosen, 0, keepdims=False)
    text_cols_w = lax.dynamic_index_in_dim(out_text, chosen, 0, keepdims=False)
    video_proj, text_proj, video_back, text_back = (
        lax.all_gather(qkv_video[0], "blk", axis=0, tiled=True),
        lax.all_gather(text_rows_w, "blk", axis=0, tiled=True),
        lax.all_gather(out_video[0], "blk", axis=1, tiled=True),
        lax.all_gather(text_cols_w, "blk", axis=1, tiled=True),
    )
    video_proj = video_proj.reshape(width, 3 * local_width)
    text_proj = text_proj.reshape(width, 3 * local_width)
    mods = modulation[0]
    gains = qk_gain[0]
    stale = stale_kv[0]
    valid_text = text_len[0]
    cache_keys = stale[0]
    cache_values = stale[1]
    places = jnp.arange(micro * sections, dtype=jnp.int32)
    key_ok = (places >= text_count) | (places < valid_text)
    carried = jnp.zeros((rows, width), jnp.bfloat16)
    inbox = hidden_in[0]
    outbox = jnp.zeros((rows, width), jnp.bfloat16)
    last_tick = 2 * sections - 2
    for tick in range(2 * sections - 1):
        micro_index = tick - section
        valid = (micro_index >= 0) & (micro_index < sections)
        current = jnp.clip(micro_index, 0, sections - 1)
        entering = jnp.where(section == 0, inbox, carried)
        is_text = dual & (current * micro + blk_index * group < text_count)
        stream = is_text.astype(jnp.int32)
        mod_rows = lax.dynamic_index_in_dim(mods, stream, 0, keepdims=False)
        gain_rows = lax.dynamic_index_in_dim(gains, stream, 0, keepdims=False)
        floats = entering.astype(jnp.float32)
        centred = floats - jnp.mean(floats, axis=-1, keepdims=True)
        normed = centred * lax.rsqrt(jnp.mean(centred * centred, axis=-1, keepdims=True) + 1e-06)
        modded = (normed * (1.0 + mod_rows[1]) + mod_rows[0]).astype(jnp.bfloat16)
        gathered = lax.all_gather(modded, "uly", axis=0, tiled=True)
        projected = lax.cond(
            is_text,
            lambda operand: jnp.dot(operand, text_proj, preferred_element_type=jnp.float32),
            lambda operand: jnp.dot(operand, video_proj, preferred_element_type=jnp.float32),
            gathered,
        )
        projected = projected.reshape(group, 3, local_heads, head_dim)
        queries = rms_scale(projected[:, 0], gain_rows[0]).astype(jnp.bfloat16)
        fresh_keys = (
            rms_scale(projected[:, 1], gain_rows[1])
            .astype(jnp.bfloat16)
            .reshape(group, local_width)
        )
        fresh_values = projected[:, 2].astype(jnp.bfloat16).reshape(group, local_width)
        all_keys, all_values = (
            lax.all_gather(fresh_keys, "blk", axis=0, tiled=True),
            lax.all_gather(fresh_values, "blk", axis=0, tiled=True),
        )
        offset = current * micro
        old_keys = lax.dynamic_slice_in_dim(cache_keys, offset, micro, 0)
        old_values = lax.dynamic_slice_in_dim(cache_values, offset, micro, 0)
        cache_keys = lax.dynamic_update_slice_in_dim(
            cache_keys, jnp.where(valid, all_keys, old_keys), offset, 0
        )
        cache_values = lax.dynamic_update_slice_in_dim(
            cache_values, jnp.where(valid, all_values, old_values), offset, 0
        )
        key_heads = cache_keys.reshape(-1, local_heads, head_dim)
        value_heads = cache_values.reshape(-1, local_heads, head_dim)
        scores = (
            jnp.einsum("rhd,lhd->hrl", queries, key_heads, preferred_element_type=jnp.float32)
            * inv_scale
        )
        scores = jnp.where(key_ok[None, None, :], scores, -1e30)
        peak = jnp.max(scores, axis=-1, keepdims=True)
        weights = jnp.where(key_ok[None, None, :], jnp.exp(scores - peak), 0.0)
        total = jnp.sum(weights, axis=-1)
        mixed = jnp.einsum(
            "hrl,lhd->rhd",
            weights.astype(jnp.bfloat16),
            value_heads,
            preferred_element_type=jnp.float32,
        )
        attended = (
            (mixed / jnp.transpose(total)[:, :, None])
            .reshape(group, local_width)
            .astype(jnp.bfloat16)
        )
        partial_value = lax.cond(
            is_text,
            lambda operand: jnp.dot(operand, text_back, preferred_element_type=jnp.float32),
            lambda operand: jnp.dot(operand, video_back, preferred_element_type=jnp.float32),
            attended,
        )
        summed = lax.psum_scatter(partial_value, "uly", scatter_dimension=0, tiled=True)
        leaving = (floats + mod_rows[2] * summed).astype(jnp.bfloat16)
        outbox = jnp.where((section == sections - 1) & valid, leaving, outbox)
        if tick < last_tick:
            carried = from_behind(leaving, "pipe", 1)
            inbox, outbox = from_behind((inbox, outbox), "pipe", -1)
    return outbox[None]


def solution(mesh):
    shape = mesh.shape
    small = shape["blk"] == 2 and shape["uly"] == 4 and shape["pipe"] == 4
    return jax.shard_map(
        fused if small else local,
        mesh=mesh,
        in_specs=(
            P("pipe", ("blk", "uly"), None),
            P(),
            P("pipe", "blk", None, "uly"),
            P(None, "blk", None, "uly"),
            P("pipe", "uly", "blk"),
            P(None, "uly", "blk"),
            P("pipe", None, None, None),
            P("pipe", None, None, None),
            P("pipe", None, None, "uly"),
        ),
        out_specs=P("pipe", ("blk", "uly"), None),
        check_vma=False,
    )
```

```python
import functools
import math

import jax
import jax.numpy as jnp
from jax import lax
from jax.experimental import pallas as pl
from jax.experimental.pallas import tpu as pltpu
from jax.sharding import PartitionSpec as P

MESH = pl.DeviceIdType.MESH


def unslab(value):
    count, _, half = value.shape
    joined = jnp.concatenate([value[:, :8], value[:, 8:]], axis=2)
    return joined.reshape(count * 8, 2 * half)


def slab(value):
    rows, width = value.shape
    split = value.reshape(rows // 8, 8, width)
    return jnp.concatenate([split[:, :, : width // 2], split[:, :, width // 2 :]], axis=1)


def pipe_kernel(
    sections, dual_count, heads, head_dim,
    len_ref, hin_ref, mod_ref, gain_ref, wqv_ref, wqt_ref, wov_ref, wot_ref, stale_ref,
    out_ref,
    mods, gains, hid, hnew, obuf, stat_first, stat_out, stat_in, part_own, part_out, part_in, y_own, y_out, y_in,
    wq, wo, kv,
    init_sem, hid_sem, fwd_sem, first_sem, stat_ssem, stat_rsem, part_ssem, part_rsem, y_ssem, y_rsem,
    next_sem, out_sem, wq_sem, wo_sem, kv_sem,
):
    s = lax.axis_index("pipe")
    i = lax.axis_index("blk")
    j = lax.axis_index("uly")
    me = (s * 2 + i) * 4 + j
    local_width = heads * head_dim
    half = mods.shape[2]
    micro = 64
    inv_scale = 1.0 / math.sqrt(head_dim)
    last = sections - 1

    barrier = pltpu.get_barrier_semaphore()
    devices = sections * 8
    for d in range(devices):
        @pl.when(d != me)
        def _():
            pl.semaphore_signal(
                barrier, inc=1, device_id=(d // 8, (d // 4) % 2, d % 4), device_id_type=MESH
            )

    chosen = jnp.minimum(s, dual_count - 1)
    edges = [0, 256, 2 * local_width, 3 * local_width]
    chunks = list(zip(edges[:-1], edges[1:]))

    def weight_copy(source, slot, c):
        return pltpu.make_async_copy(
            source, wq.at[slot, :, pl.ds(c * local_width, local_width)], wq_sem.at[slot, c]
        )

    for c in range(3):
        @pl.when(s < dual_count)
        def _():
            weight_copy(wqt_ref.at[chosen, c], 0, c).start()

        @pl.when(s >= dual_count)
        def _():
            weight_copy(wqv_ref.at[c], 0, c).start()

    @pl.when(s < dual_count)
    def _():
        pltpu.make_async_copy(wot_ref.at[chosen], wo.at[0], wo_sem.at[0]).start()

    @pl.when(s >= dual_count)
    def _():
        pltpu.make_async_copy(wov_ref, wo.at[0], wo_sem.at[0]).start()

    pltpu.make_async_copy(stale_ref, kv, kv_sem.at[0]).start()
    for c in range(3):
        weight_copy(wqv_ref.at[c], 1, c).start()
    pltpu.make_async_copy(wov_ref, wo.at[1], wo_sem.at[1]).start()

    dual = s < dual_count
    cols = pl.ds(pl.multiple_of(i * half, 128), half)
    for k in range(3):
        video, text = mod_ref[k, 0:1, cols], mod_ref[k, 1:2, cols]
        mods[0, k : k + 1, :] = jnp.where(dual, text, video)
        mods[1, k : k + 1, :] = video
    gains[1] = gain_ref[0]
    gains[0] = jnp.where(dual, gain_ref[1], gain_ref[0])

    def stats_of(floats):
        mean = jnp.mean(floats, axis=-1, keepdims=True)
        centred = floats - mean
        spread = jnp.sum(centred * centred, axis=-1, keepdims=True)
        return mean, spread

    def packed_stats(floats):
        mean, spread = stats_of(floats)
        lanes = lax.broadcasted_iota(jnp.int32, (floats.shape[0], 128), 1)
        return jnp.where(lanes < 64, mean, spread).reshape(-1, 8, 128)

    for side in range(2):
        stat_first[side] = packed_stats(unslab(hin_ref[side : side + 1].astype(jnp.float32)))[0]

    pl.semaphore_wait(barrier, devices - 1)

    def init_target(k):
        return 4 * (k // 2) + 2 * (k % 2) + j // 2

    def init_copy(k):
        return pltpu.make_async_remote_copy(
            src_ref=hin_ref.at[k // 2],
            dst_ref=hid.at[s, i * 4 + j],
            send_sem=init_sem.at[k],
            recv_sem=hid_sem.at[s, i * 4 + j],
            device_id=(0, k // 2, 2 * (k % 2) + j // 2),
            device_id_type=MESH,
        )

    def first_copy(k):
        return pltpu.make_async_remote_copy(
            src_ref=stat_first.at[1 - k // 4],
            dst_ref=stat_in.at[s, i * 4 + j],
            send_sem=first_sem.at[k],
            recv_sem=stat_rsem.at[s, i * 4 + j],
            device_id=(0, k // 4, k % 4),
            device_id_type=MESH,
        )

    for k in range(4):
        @pl.when(me != init_target(k))
        def _():
            init_copy(k).start()

        @pl.when(me == init_target(k))
        def _():
            pltpu.make_async_copy(
                hin_ref.at[k // 2], hid.at[s, i * 4 + j], hid_sem.at[s, i * 4 + j]
            ).start()

    for k in range(8):
        @pl.when(me != k)
        def _():
            first_copy(k).start()

        @pl.when(me == k)
        def _():
            pltpu.make_async_copy(
                stat_first.at[1 - k // 4], stat_in.at[s, i * 4 + j], stat_rsem.at[s, i * 4 + j]
            ).start()

    def stat_copy(m, to):
        return pltpu.make_async_remote_copy(
            src_ref=stat_out.at[m], dst_ref=stat_in.at[m, pl.ds(2 * j, 2)],
            send_sem=stat_ssem.at[m, to], recv_sem=stat_rsem.at[m, j],
            device_id=(s + 1, 1 - i, to), device_id_type=MESH,
        )

    def part_copy(m, c):
        return pltpu.make_async_remote_copy(
            src_ref=part_out.at[m, :, pl.ds(chunks[c][0], chunks[c][1] - chunks[c][0])],
            dst_ref=part_in.at[m, :, pl.ds(chunks[c][0], chunks[c][1] - chunks[c][0])],
            send_sem=part_ssem.at[m, c], recv_sem=part_rsem.at[m, c],
            device_id=(s, 1 - i, j), device_id_type=MESH,
        )

    def y_copy(m, o, e):
        to = (j + o) % 4
        slot = 2 * (o - 1) + e
        return pltpu.make_async_remote_copy(
            src_ref=y_out.at[m, 2 * to + e], dst_ref=y_in.at[m, slot],
            send_sem=y_ssem.at[m, slot], recv_sem=y_rsem.at[m, slot],
            device_id=(s, i, to), device_id_type=MESH,
        )

    parity = j % 2

    def next_copy(m, e, side):
        return pltpu.make_async_remote_copy(
            src_ref=hnew.at[m, e], dst_ref=hid.at[m, 2 * j + e],
            send_sem=next_sem.at[m, 2 * e + side], recv_sem=hid_sem.at[m, 2 * j + e],
            device_id=(s + 1, i, 2 * side + parity), device_id_type=MESH,
        )

    def forward_copy(m, e, side):
        g = 2 * (2 * side + parity) + e
        return pltpu.make_async_remote_copy(
            src_ref=hid.at[m, g], dst_ref=hid.at[m, g],
            send_sem=fwd_sem.at[m, 2 * e + side], recv_sem=hid_sem.at[m, g],
            device_id=(s, i, j + 1 - 2 * parity), device_id_type=MESH,
        )

    def out_copy(m, e):
        g = 2 * j + e
        return pltpu.make_async_remote_copy(
            src_ref=hnew.at[m, e], dst_ref=obuf.at[i],
            send_sem=next_sem.at[m, e], recv_sem=out_sem.at[i],
            device_id=(m, g // 4, g % 4), device_id_type=MESH,
        )

    def owner(m, e):
        return m * 8 + 2 * j + e

    def arrive(m):
        def take(ref, sem):
            pltpu.make_async_copy(ref, ref, sem).wait()

        for e in range(2):
            for side in range(2):
                g = 2 * (2 * side + parity) + e
                take(hid.at[m, g], hid_sem.at[m, g])
                forward_copy(m, e, side).start()
        for e in range(2):
            for side in range(2):
                g = 2 * (2 * side + 1 - parity) + e
                take(hid.at[m, g], hid_sem.at[m, g])

        @pl.when(s == 0)
        def _():
            for r in range(8):
                take(stat_in.at[m, r], stat_rsem.at[m, r])

        @pl.when(s > 0)
        def _():
            for r in range(4):
                take(stat_in.at[m, pl.ds(2 * r, 2)], stat_rsem.at[m, r])

    def stage_b(m, sel):
        arrive(m)
        floats = unslab(hid[m].astype(jnp.float32))
        mean_a, spread_a = stats_of(floats)
        other = stat_in[m].reshape(micro, 128)
        mean_b, spread_b = other[:, 0:1], other[:, 64:65]
        mean = 0.5 * (mean_a + mean_b)
        delta = mean_a - mean_b
        var = (spread_a + spread_b + delta * delta * (0.5 * half)) / (2 * half)
        scale = 1.0 + mods[sel, 1:2, :]
        shift = mods[sel, 0:1, :]
        normed = (floats - mean) * lax.rsqrt(var + 1e-06)
        modded = (normed * scale + shift).astype(jnp.bfloat16)

        @pl.when(m < 2)
        def _():
            for c in range(3):
                weight_copy(wqv_ref.at[c], sel, c).wait()

        for c, (lo, hi) in enumerate(chunks):
            part = jnp.dot(modded, wq[sel, :, lo:hi], preferred_element_type=jnp.float32)
            part_own[m % 2, :, lo:hi] = part
            part_out[m, :, lo:hi] = part.astype(jnp.bfloat16)
            part_copy(m, c).start()

    def stage_c(m, sel):
        early = [c for c in range(len(chunks)) if chunks[c][0] < 2 * local_width]
        for c in early:
            part_copy(m, c).wait_recv()

        def take(c):
            lo, hi = c * local_width, (c + 1) * local_width
            return part_own[m % 2, :, lo:hi] + part_in[m, :, lo:hi].astype(jnp.float32)

        def norm(value, gain):
            pieces = []
            for h in range(heads):
                one = value[:, h * head_dim : (h + 1) * head_dim]
                squares = jnp.mean(one * one, axis=-1, keepdims=True)
                pieces.append((one * lax.rsqrt(squares + 1e-06) * gain).astype(jnp.bfloat16))
            return pieces

        @pl.when(m == 0)
        def _():
            pltpu.make_async_copy(stale_ref, kv, kv_sem.at[0]).wait()

        @pl.when(m < 2)
        def _():
            pltpu.make_async_copy(wov_ref, wo.at[sel], wo_sem.at[sel]).wait()

        queries = norm(take(0), gains[sel, 0:1, :])
        kv[0, m] = jnp.concatenate(norm(take(1), gains[sel, 1:2, :]), axis=1)
        places = lax.broadcasted_iota(jnp.int32, (1, sections * micro), 1)
        bias = jnp.where((places >= micro) | (places < len_ref[0]), 0.0, -1e30)
        raised = []
        for h in range(heads):
            cols = slice(h * head_dim, (h + 1) * head_dim)
            keys = kv[0, :, :, cols].reshape(sections * micro, head_dim)
            scores = lax.dot_general(
                queries[h], keys, (((1,), (1,)), ((), ())), preferred_element_type=jnp.float32
            )
            scores = scores * inv_scale + bias
            peak = jnp.max(scores, axis=-1, keepdims=True)
            weights = jnp.exp(scores - peak)
            total = jnp.sum(weights, axis=-1, keepdims=True)
            raised.append((weights.astype(jnp.bfloat16), total))
        for c in range(len(early), len(chunks)):
            part_copy(m, c).wait_recv()
        kv[1, m] = take(2).astype(jnp.bfloat16)
        outs = []
        for h, (weights, total) in enumerate(raised):
            cols = slice(h * head_dim, (h + 1) * head_dim)
            values = kv[1, :, :, cols].reshape(sections * micro, head_dim)
            mixed = jnp.dot(weights, values, preferred_element_type=jnp.float32)
            outs.append((mixed * (1.0 / total)).astype(jnp.bfloat16))
        attended = jnp.concatenate(outs, axis=1)
        y = slab(jnp.dot(attended, wo[sel], preferred_element_type=jnp.float32))
        y_own[...] = y
        y_out[m] = y.astype(jnp.bfloat16)
        for e in range(2):
            for o in (2, 3, 1):
                y_copy(m, o, e).start()

    def stage_d(m, sel):
        gate = mods[sel, 2:3, :]
        gate = slab(jnp.broadcast_to(gate, (8, half)))[0]
        for e in range(2):
            total = y_own[2 * j + e]
            for o in (1, 2, 3):
                y_copy(m, o, e).wait_recv()
                total = total + y_in[m, 2 * (o - 1) + e].astype(jnp.float32)
            old = hid[m, 2 * j + e].astype(jnp.float32)
            hnew[m, e] = (old + gate * total).astype(jnp.bfloat16)

            @pl.when(s < last)
            def _():
                for side in range(2):
                    next_copy(m, e, side).start()

            @pl.when(s == last)
            def _():
                @pl.when(me != owner(m, e))
                def _():
                    out_copy(m, e).start()

                @pl.when(me == owner(m, e))
                def _():
                    pltpu.make_async_copy(hnew.at[m, e], obuf.at[i], out_sem.at[i]).start()

        @pl.when(s < last)
        def _():
            stat_out[m] = packed_stats(unslab(hnew[m].astype(jnp.float32)))
            for to in range(4):
                stat_copy(m, to).start()

    stage_b(0, 0)

    @pl.loop(0, sections)
    def _(m):
        sel = jnp.minimum(m, 1)
        stage_c(m, sel)

        @pl.when(m < last)
        def _():
            stage_b(m + 1, 1)

        stage_d(m, sel)

    for k in range(4):
        @pl.when(me != init_target(k))
        def _():
            init_copy(k).wait_send()

    for k in range(8):
        @pl.when(me != k)
        def _():
            first_copy(k).wait_send()

    @pl.loop(0, sections)
    def _(m):
        for c in range(len(chunks)):
            part_copy(m, c).wait_send()
        for e in range(2):
            for o in (1, 2, 3):
                y_copy(m, o, e).wait_send()

        for e in range(2):
            for side in range(2):
                forward_copy(m, e, side).wait_send()

        @pl.when(s < last)
        def _():
            for e in range(2):
                for side in range(2):
                    next_copy(m, e, side).wait_send()
            for to in range(4):
                stat_copy(m, to).wait_send()

        @pl.when(s == last)
        def _():
            for e in range(2):
                @pl.when(me != owner(m, e))
                def _():
                    out_copy(m, e).wait_send()

    for side in range(2):
        pltpu.make_async_copy(obuf.at[side], obuf.at[side], out_sem.at[side]).wait()
    out_ref[...] = obuf[...]


def fused(
    hidden_in, text_len, qkv_video, qkv_text, out_video, out_text, modulation, qk_gain, stale_kv
):
    sections = lax.axis_size("pipe")
    rows, width = hidden_in.shape[1:]
    half = width // 2
    micro = rows * 8
    dual_count = qkv_text.shape[0]
    head_dim = qk_gain.shape[3]
    local_width = stale_kv.shape[3]
    heads = local_width // head_dim
    wqv = jnp.transpose(qkv_video[0], (1, 0, 2))
    wqt = jnp.transpose(qkv_text, (0, 2, 1, 3))
    mods = jnp.transpose(modulation[0], (1, 0, 2))
    stale = stale_kv[0].reshape(2, sections, micro, local_width)
    quarter = half // 2
    hin = hidden_in[0].reshape(rows, 2, 2, quarter)
    hin = jnp.transpose(hin, (1, 2, 0, 3)).reshape(2, 2 * rows, quarter)
    pieces = 3
    bf16, f32 = jnp.bfloat16, jnp.float32
    dma = pltpu.SemaphoreType.DMA
    vmem = pl.BlockSpec(memory_space=pltpu.VMEM)
    anyspace = pl.BlockSpec(memory_space=pl.ANY)
    out = pl.pallas_call(
        functools.partial(pipe_kernel, sections, dual_count, heads, head_dim),
        out_shape=jax.ShapeDtypeStruct((2, 2 * rows, quarter), bf16),
        in_specs=[pl.BlockSpec(memory_space=pltpu.SMEM)] + [vmem] * 3 + [anyspace] * 5,
        out_specs=vmem,
        scratch_shapes=[
            pltpu.VMEM((2, 3, half), f32),
            pltpu.VMEM((2, 2, head_dim), f32),
            pltpu.VMEM((sections, 8, 2 * rows, quarter), bf16),
            pltpu.VMEM((sections, 2, 2 * rows, quarter), bf16),
            pltpu.VMEM((2, 2 * rows, quarter), bf16),
            pltpu.VMEM((2, 8, 128), f32),
            pltpu.VMEM((sections, 2, 8, 128), f32),
            pltpu.VMEM((sections, 8, 8, 128), f32),
            pltpu.VMEM((2, micro, 3 * local_width), f32),
            pltpu.VMEM((sections, micro, 3 * local_width), bf16),
            pltpu.VMEM((sections, micro, 3 * local_width), bf16),
            pltpu.VMEM((8, 2 * rows, quarter), f32),
            pltpu.VMEM((sections, 8, 2 * rows, quarter), bf16),
            pltpu.VMEM((sections, 6, 2 * rows, quarter), bf16),
            pltpu.VMEM((2, half, 3 * local_width), bf16),
            pltpu.VMEM((2, local_width, half), bf16),
            pltpu.VMEM((2, sections, micro, local_width), bf16),
            dma((4,)),
            dma((sections, 8)),
            dma((sections, 4)),
            dma((8,)),
            dma((sections, 4)),
            dma((sections, 8)),
            dma((sections, pieces)),
            dma((sections, pieces)),
            dma((sections, 6)),
            dma((sections, 6)),
            dma((sections, 4)),
            dma((2,)),
            dma((2, 3)),
            dma((2,)),
            dma((1,)),
        ],
        compiler_params=pltpu.CompilerParams(
            collective_id=0, has_side_effects=True, vmem_limit_bytes=60 * 1024 * 1024
        ),
        cost_estimate=pl.CostEstimate(
            flops=8 * micro * sections * half * local_width,
            bytes_accessed=16 * half * local_width,
            transcendentals=heads * micro * sections * micro * sections,
        ),
    )(text_len, hin, mods, qk_gain[0], wqv, wqt, out_video[0], out_text, stale)
    out = out.reshape(2, 2, rows, quarter)
    return jnp.transpose(out, (2, 0, 1, 3)).reshape(1, rows, width)


def from_behind(shard, axis, by):
    size = lax.axis_size(axis)
    pairs = [(i, i + by) for i in range(size) if 0 <= i + by < size]
    return lax.ppermute(shard, axis, pairs)


def rms_scale(values, gain):
    squares = jnp.mean(values * values, axis=-1, keepdims=True)
    return values * lax.rsqrt(squares + 1e-06) * gain


def local(
    hidden_in, text_len, qkv_video, qkv_text, out_video, out_text, modulation, qk_gain, stale_kv
):
    sections = lax.axis_size("pipe")
    blk_count = lax.axis_size("blk")
    uly_count = lax.axis_size("uly")
    section = lax.axis_index("pipe")
    blk_index = lax.axis_index("blk")
    rows = hidden_in.shape[1]
    width = hidden_in.shape[2]
    group = rows * uly_count
    micro = group * blk_count
    text_count = 2 * group
    dual_count = qkv_text.shape[0]
    head_dim = qk_gain.shape[3]
    local_width = stale_kv.shape[3]
    local_heads = local_width // head_dim
    inv_scale = 1.0 / math.sqrt(head_dim)
    dual = section < dual_count
    chosen = jnp.minimum(section, dual_count - 1)
    text_rows_w = lax.dynamic_index_in_dim(qkv_text, chosen, 0, keepdims=False)
    text_cols_w = lax.dynamic_index_in_dim(out_text, chosen, 0, keepdims=False)
    video_proj, text_proj, video_back, text_back = (
        lax.all_gather(qkv_video[0], "blk", axis=0, tiled=True),
        lax.all_gather(text_rows_w, "blk", axis=0, tiled=True),
        lax.all_gather(out_video[0], "blk", axis=1, tiled=True),
        lax.all_gather(text_cols_w, "blk", axis=1, tiled=True),
    )
    video_proj = video_proj.reshape(width, 3 * local_width)
    text_proj = text_proj.reshape(width, 3 * local_width)
    mods = modulation[0]
    gains = qk_gain[0]
    stale = stale_kv[0]
    valid_text = text_len[0]
    cache_keys = stale[0]
    cache_values = stale[1]
    places = jnp.arange(micro * sections, dtype=jnp.int32)
    key_ok = (places >= text_count) | (places < valid_text)
    carried = jnp.zeros((rows, width), jnp.bfloat16)
    inbox = hidden_in[0]
    outbox = jnp.zeros((rows, width), jnp.bfloat16)
    last_tick = 2 * sections - 2
    for tick in range(2 * sections - 1):
        micro_index = tick - section
        valid = (micro_index >= 0) & (micro_index < sections)
        current = jnp.clip(micro_index, 0, sections - 1)
        entering = jnp.where(section == 0, inbox, carried)
        is_text = dual & (current * micro + blk_index * group < text_count)
        stream = is_text.astype(jnp.int32)
        mod_rows = lax.dynamic_index_in_dim(mods, stream, 0, keepdims=False)
        gain_rows = lax.dynamic_index_in_dim(gains, stream, 0, keepdims=False)
        floats = entering.astype(jnp.float32)
        centred = floats - jnp.mean(floats, axis=-1, keepdims=True)
        normed = centred * lax.rsqrt(jnp.mean(centred * centred, axis=-1, keepdims=True) + 1e-06)
        modded = (normed * (1.0 + mod_rows[1]) + mod_rows[0]).astype(jnp.bfloat16)
        gathered = lax.all_gather(modded, "uly", axis=0, tiled=True)
        projected = lax.cond(
            is_text,
            lambda operand: jnp.dot(operand, text_proj, preferred_element_type=jnp.float32),
            lambda operand: jnp.dot(operand, video_proj, preferred_element_type=jnp.float32),
            gathered,
        )
        projected = projected.reshape(group, 3, local_heads, head_dim)
        queries = rms_scale(projected[:, 0], gain_rows[0]).astype(jnp.bfloat16)
        fresh_keys = (
            rms_scale(projected[:, 1], gain_rows[1])
            .astype(jnp.bfloat16)
            .reshape(group, local_width)
        )
        fresh_values = projected[:, 2].astype(jnp.bfloat16).reshape(group, local_width)
        all_keys, all_values = (
            lax.all_gather(fresh_keys, "blk", axis=0, tiled=True),
            lax.all_gather(fresh_values, "blk", axis=0, tiled=True),
        )
        offset = current * micro
        old_keys = lax.dynamic_slice_in_dim(cache_keys, offset, micro, 0)
        old_values = lax.dynamic_slice_in_dim(cache_values, offset, micro, 0)
        cache_keys = lax.dynamic_update_slice_in_dim(
            cache_keys, jnp.where(valid, all_keys, old_keys), offset, 0
        )
        cache_values = lax.dynamic_update_slice_in_dim(
            cache_values, jnp.where(valid, all_values, old_values), offset, 0
        )
        key_heads = cache_keys.reshape(-1, local_heads, head_dim)
        value_heads = cache_values.reshape(-1, local_heads, head_dim)
        scores = (
            jnp.einsum("rhd,lhd->hrl", queries, key_heads, preferred_element_type=jnp.float32)
            * inv_scale
        )
        scores = jnp.where(key_ok[None, None, :], scores, -1e30)
        peak = jnp.max(scores, axis=-1, keepdims=True)
        weights = jnp.where(key_ok[None, None, :], jnp.exp(scores - peak), 0.0)
        total = jnp.sum(weights, axis=-1)
        mixed = jnp.einsum(
            "hrl,lhd->rhd",
            weights.astype(jnp.bfloat16),
            value_heads,
            preferred_element_type=jnp.float32,
        )
        attended = (
            (mixed / jnp.transpose(total)[:, :, None])
            .reshape(group, local_width)
            .astype(jnp.bfloat16)
        )
        partial_value = lax.cond(
            is_text,
            lambda operand: jnp.dot(operand, text_back, preferred_element_type=jnp.float32),
            lambda operand: jnp.dot(operand, video_back, preferred_element_type=jnp.float32),
            attended,
        )
        summed = lax.psum_scatter(partial_value, "uly", scatter_dimension=0, tiled=True)
        leaving = (floats + mod_rows[2] * summed).astype(jnp.bfloat16)
        outbox = jnp.where((section == sections - 1) & valid, leaving, outbox)
        if tick < last_tick:
            carried = from_behind(leaving, "pipe", 1)
            inbox, outbox = from_behind((inbox, outbox), "pipe", -1)
    return outbox[None]


def solution(mesh):
    shape = mesh.shape
    small = shape["blk"] == 2 and shape["uly"] == 4 and shape["pipe"] == 4
    return jax.shard_map(
        fused if small else local,
        mesh=mesh,
        in_specs=(
            P("pipe", ("blk", "uly"), None),
            P(),
            P("pipe", "blk", None, "uly"),
            P(None, "blk", None, "uly"),
            P("pipe", "uly", "blk"),
            P(None, "uly", "blk"),
            P("pipe", None, None, None),
            P("pipe", None, None, None),
            P("pipe", None, None, "uly"),
        ),
        out_specs=P("pipe", ("blk", "uly"), None),
        check_vma=False,
    )
```
